32 devices in a mesh: groups: 2 (over y), scan: 4 (over z), mode: 2 (over x), sub: 2 (over core).
Axes of the slice: x: 2, y: 2, z: 4, core: 2. Of those that a mesh axis runs over, the one named last changes fastest.
Arguments:
- object_field: float32 [2, 2048, 1024], P(None, ('groups', 'scan')), parts along dimension 1, may hold values from -6 to 6
- probe: float32 [8, 2, 256, 256], P('mode', None, 'sub'), may hold values from -3 to 3
- offsets: int32 [8, 4, 2], P(('groups', 'scan')), parts along dimension 0, may hold values from 0 to 768, as said below
- counts: int32 [8], P(('groups', 'scan')), parts along dimension 0, may hold values from 1 to 4, as said below
- measured: float32 [8, 4, 256, 256], P(('groups', 'scan'), None, None, 'sub'), parts along dimension 0, may hold values from 0.25 to 16
Outputs:
- object_grad: float32 [2, 2048, 1024], P(None, ('groups', 'scan'), ('mode', 'sub')), parts along dimension 1
- probe_grad: float32 [16, 2, 256, 256], P(('groups', 'mode'), None, 'sub'), parts along dimension 0
The draws below stay inside these ranges and needn't reach their ends.
There are 2 independent parts, one for each index of `groups`. The reference program is written for one: setup_inputs(seed, part) draws one part's arguments, and reference() takes and returns one part's arrays. A program takes and returns all parts, laid end to end along the dimension named above; an argument that names none is the same for every part. Nothing has to cross between parts.
Inputs may be any that keep to these rules, and one draw needn't show every extreme that they name: Every slot's row offset on tile t lies between t * 256 and t * 256 + 128, and is exactly t * 256 on the last tile; column offsets lie between 0 and 768; some slot reaches each end of both ranges; slots that are not live hold valid offsets too. `counts`: some tile has all 4 slots live.
All inputs are finite; a program needn't handle non-finite values.
Results may differ from the reference program's by a relative error of at most 0.0001.
Values sent between devices are 32-bit elements; how exact they have to be, the bound alone decides.
A program may use at most 64 MiB of HBM per device.

```python
import math
import jax
import jax.numpy as jnp
from jax import lax

FRAME = 256
MODES = 8
CAP = 4
TILE_R = 256
OBJ_C = 1024
HALO = 128
TILES = 4
OBJ_R = 1024


def draw_offsets(key, part):
    key = jax.random.fold_in(key, 11)
    row_key, col_key = jax.random.split(key)
    rel_rows = jax.random.randint(row_key, (TILES, CAP), 0, HALO + 1)
    tile_ids = jnp.arange(TILES, dtype=jnp.int32)[:, None]
    slot_ids = jnp.arange(CAP, dtype=jnp.int32)[None, :]
    rel_rows = jnp.where((tile_ids == 0) & (slot_ids == 0), HALO, rel_rows)
    rel_rows = jnp.where(tile_ids == TILES - 1, 0, rel_rows)
    col_starts = jax.random.randint(col_key, (TILES, CAP), 0, OBJ_C - FRAME + 1)
    col_starts = jnp.where((tile_ids == 1) & (slot_ids == 0), OBJ_C - FRAME, col_starts)
    col_starts = jnp.where((tile_ids == 0) & (slot_ids == 1), 0, col_starts)
    return jnp.stack([tile_ids * TILE_R + rel_rows, col_starts], axis=-1).astype(jnp.int32)


def draw_counts(key, part):
    key = jax.random.fold_in(key, 12)
    count_key, full_key = jax.random.split(key)
    values = jax.random.randint(count_key, (TILES,), 1, CAP + 1)
    full_tile = jax.random.randint(full_key, (), 0, TILES)
    values = jnp.where(jnp.arange(TILES) == full_tile, CAP, values)
    return values.astype(jnp.int32)


def level_of(rng, shape, cuts, smallest, top_value):
    loudness, own = 1.0, jax.random.fold_in(rng, 6)
    for position, parts in cuts:
        draws = jnp.exp(jax.random.uniform(jax.random.fold_in(own, position), (parts,), jnp.float32, smallest / len(cuts), top_value / len(cuts)))
        loudness = loudness * jnp.repeat(draws, shape[position] // parts).reshape([-1 if axis == position else 1 for axis in range(len(shape))])
    return loudness


def noise(stream_key, shape, spread, limit, pieces=(), kind=jnp.bfloat16):
    array = jax.random.normal(stream_key, shape, jnp.float32) * spread
    if len(pieces) > 0:
        array = level_of(stream_key, shape, pieces, -0.22, 0.18) * array
    return jnp.clip(array, min=-limit, max=limit).astype(kind)


def setup_inputs(seed: int = 0, part: int = 0) -> dict:
    keys = jax.random.split(jax.random.key(seed), 6)
    part_keys = jax.random.split(jax.random.fold_in(keys[5], part), 6)
    object_field = noise(part_keys[0], (2, OBJ_R, OBJ_C), 1.0, 6.0, ((1, 4),), jnp.float32)
    probe = noise(keys[1], (MODES, 2, FRAME, FRAME), 0.5, 3.0, ((0, 2), (2, 2)), jnp.float32)
    offsets = draw_offsets(jax.random.fold_in(jax.random.fold_in(keys[5], part), 71), part)
    counts = draw_counts(jax.random.fold_in(jax.random.fold_in(keys[5], part), 71), part)
    measured = jnp.clip(jnp.exp(math.log(16.0) - 4.158883 * jax.random.uniform(part_keys[4], (TILES, CAP, FRAME, FRAME), jnp.float32) ** level_of(part_keys[4], (TILES, CAP, FRAME, FRAME), ((0, 4), (3, 2)), -0.2, 0.2)), 0.25, 16.0)
    return {"object_field": object_field, "probe": probe, "offsets": offsets, "counts": counts, "measured": measured}


def reference(object_field, probe, offsets, counts, measured):
    object_map = object_field[0] + 1j * object_field[1]
    probe_map = probe[:, 0] + 1j * probe[:, 1]
    flat_offsets = offsets.reshape(TILES * CAP, 2)
    live_slot = (jnp.arange(CAP, dtype=jnp.int32)[None, :] < counts[:, None]).astype(jnp.float32).reshape(TILES * CAP)
    flat_measured = measured.reshape(TILES * CAP, FRAME, FRAME)

    def visit(carry, item):
        object_total, probe_total = carry
        offset_pair, measured_frame, weight = item
        patch = lax.dynamic_slice(object_map, (offset_pair[0], offset_pair[1]), (FRAME, FRAME))
        spectra = jnp.fft.fft2(probe_map * patch[None], norm='ortho')
        intensity = lax.optimization_barrier(jnp.sum(jnp.real(spectra) ** 2 + jnp.imag(spectra) ** 2, axis=0))
        scaling = weight * (1.0 - jnp.sqrt(measured_frame + 1.0) / jnp.sqrt(intensity + 1.0))
        chi_field = jnp.fft.ifft2(spectra * scaling[None], norm='ortho')
        object_term = lax.optimization_barrier(jnp.sum(jnp.conj(probe_map) * chi_field, axis=0))
        current = lax.dynamic_slice(object_total, (offset_pair[0], offset_pair[1]), (FRAME, FRAME))
        object_total = lax.dynamic_update_slice(object_total, current + object_term, (offset_pair[0], offset_pair[1]))
        probe_total = probe_total + jnp.conj(patch)[None] * chi_field
        return ((object_total, probe_total), None)
    start_object = jnp.zeros((OBJ_R, OBJ_C), jnp.float32) * object_map[0, 0] * 0.0
    start_probe = jnp.zeros((MODES, FRAME, FRAME), jnp.float32) * probe_map[0, 0, 0] * 0.0
    (object_total, probe_total), unused = lax.scan(visit, (start_object, start_probe), (flat_offsets, flat_measured, live_slot))
    object_grad = jnp.stack([jnp.real(object_total), jnp.imag(object_total)]).astype(jnp.float32)
    probe_total = probe_total / TILES
    probe_grad = jnp.stack([jnp.real(probe_total), jnp.imag(probe_total)], axis=1).astype(jnp.float32)
    return (object_grad, probe_grad)
```

```python
import functools
import math

import jax
import jax.numpy as jnp
import numpy as np
from jax import lax
from jax.experimental import pallas as pl
from jax.experimental.pallas import tpu as pltpu
from jax.sharding import PartitionSpec as P

HALO = 128
MESH = pl.DeviceIdType.MESH


def split_table(table):
    high = table.astype(np.float32).astype(jnp.bfloat16)
    low = (table - high.astype(np.float64)).astype(np.float32).astype(jnp.bfloat16)
    return high, low


def transform_tables(length):
    index = np.arange(length)
    angles = (index[:, None] * index[None, :] % length) * (2.0 * math.pi / length)
    cosine = np.cos(angles) / math.sqrt(length)
    sine = np.sin(angles) / math.sqrt(length)
    parts = []
    for table in (cosine, cosine + sine, cosine - sine):
        parts.extend(split_table(table))
    return np.stack(parts)


def split(x):
    high = x.astype(jnp.bfloat16)
    low = (x - high.astype(jnp.float32)).astype(jnp.bfloat16)
    return high, low


def mm(a, b):
    return jnp.dot(a, b, preferred_element_type=jnp.float32)


def mm_t(a, b):
    return lax.dot_general(a, b, (((1,), (1,)), ((), ())), preferred_element_type=jnp.float32)


def dot3(a, b):
    return mm(a[0], b[0]) + (mm(a[1], b[0]) + mm(a[0], b[1]))


def selectors(offsets, counts, tile_start, first, slots, frame, tile, obj_c):
    own = lax.dynamic_slice_in_dim(offsets[0], first, slots, axis=0)
    pixel = jnp.arange(frame, dtype=jnp.int32)
    row = (own[:, :1] - tile_start) + pixel
    col = (own[:, 1:] + pixel).reshape(1, slots * frame)
    rows = jnp.arange(tile + HALO, dtype=jnp.int32)
    cols = jnp.arange(obj_c, dtype=jnp.int32)[:, None]
    take_rows = (row[:, :, None] == rows[None, None, :]).astype(jnp.bfloat16)
    put_rows = (rows[None, :, None] == row[:, None, :]).astype(jnp.bfloat16)
    take_cols = (cols == col).astype(jnp.bfloat16)
    live = (first + jnp.arange(slots, dtype=jnp.int32) < counts[0]).astype(jnp.float32)
    return take_rows, put_rows, take_cols, jnp.broadcast_to(live[:, None, None], (slots, 1, frame))


def kernel(
    n, nm, obj, probe, take_rows, put_rows, take_cols, live, meas, tabs, og, pg,
    ext, pf, mf, q, spec, inten, inten_in, objt, pterm, px, x, p_left, p_right, tot,
    g, g_in, h, h_in, hz,
    loc_sem, probe_sem, meas_sem, halo_sem, fwd_sem, int_sem, px_sem, part_send, pl_sem, pr_sem,
    tot_out, tot_in, gs_sem, hs_sem, hz_sem,
):
    t = lax.axis_index("scan")
    mode = lax.axis_index("mode")
    sub = lax.axis_index("sub")
    sib = 1 - sub
    tile = obj.shape[1]
    obj_c = obj.shape[2]
    nk = probe.shape[0]
    cut = probe.shape[2]
    frame = probe.shape[3]
    mcols = meas.shape[3]
    slots = mf.shape[0]
    width = og.shape[2]
    half = obj_c // 2
    chunks = x.shape[0]
    owner = (n - 1) // 2

    def remote(src, dst, send, recv, **where):
        return pltpu.make_async_remote_copy(
            src_ref=src, dst_ref=dst, send_sem=send, recv_sem=recv,
            device_id=where, device_id_type=MESH,
        )

    barrier = pltpu.get_barrier_semaphore()
    pl.semaphore_signal(barrier, inc=1, device_id={"sub": sib}, device_id_type=MESH)
    for d in range(1, nm):
        pl.semaphore_signal(
            barrier, inc=1, device_id={"mode": lax.rem(mode + d, nm)}, device_id_type=MESH
        )

    @pl.when(t > 0)
    def _():
        pl.semaphore_signal(barrier, inc=1, device_id={"scan": t - 1}, device_id_type=MESH)

    @pl.when(t < n - 1)
    def _():
        pl.semaphore_signal(barrier, inc=1, device_id={"scan": t + 1}, device_id_type=MESH)

    own_obj = pltpu.make_async_copy(obj, ext.at[:, pl.ds(0, tile)], loc_sem.at[0])
    own_rows = pl.ds(pl.multiple_of(sub * cut, cut), cut)
    sib_rows = pl.ds(pl.multiple_of(sib * cut, cut), cut)
    own_probe = pltpu.make_async_copy(probe, pf.at[:, :, own_rows], loc_sem.at[1])
    own_mcols = pl.ds(pl.multiple_of(sub * mcols, mcols), mcols)
    own_meas = pltpu.make_async_copy(
        meas.at[0, pl.ds(sub * slots, slots)], mf.at[:, :, own_mcols], loc_sem.at[2]
    )
    own_obj.start()
    own_probe.start()
    own_meas.start()
    pl.semaphore_wait(
        barrier, nm + (t > 0).astype(jnp.int32) + (t < n - 1).astype(jnp.int32)
    )

    own_half = pl.ds(pl.multiple_of(sub * half, half), half)

    def halo(c):
        return remote(
            obj.at[c, pl.ds(0, HALO), own_half], ext.at[c, pl.ds(tile, HALO), own_half],
            halo_sem.at[0, c], halo_sem.at[1, c], scan=jnp.maximum(t - 1, 0),
        )

    def forwarded(c):
        part = ext.at[c, pl.ds(tile, HALO), own_half]
        return remote(part, part, fwd_sem.at[0, c], fwd_sem.at[1, c], sub=sib)

    @pl.when(t > 0)
    def _():
        halo(0).start()
        halo(1).start()

    send_probe = remote(
        probe, pf.at[:, :, own_rows], probe_sem.at[0], probe_sem.at[1], sub=sib
    )
    send_probe.start()
    send_meas = remote(
        meas.at[0, pl.ds(sib * slots, slots)], mf.at[:, :, own_mcols],
        meas_sem.at[0], meas_sem.at[1], sub=sib,
    )
    send_meas.start()

    objt[...] = jnp.zeros_like(objt)
    inten[...] = jnp.zeros_like(inten)

    @pl.when(t < n - 1)
    def _():
        for c in range(2):
            halo(c).wait_recv()
            forwarded(c).start()
        for c in range(2):
            forwarded(c).wait_send()
            forwarded(c).wait_recv()

    own_obj.wait()

    @pl.when(t == n - 1)
    def _():
        ext[:, pl.ds(tile, HALO)] = jnp.zeros((2, HALO, obj_c), jnp.float32)

    own_probe.wait()
    send_probe.wait()

    for c in range(2):
        high, low = split(ext[c])
        picked = mm(high, take_cols[...]) + mm(low, take_cols[...])
        for s in range(slots):
            high, low = split(picked[:, s * frame : (s + 1) * frame])
            q[s, c] = mm(take_rows[s], high) + mm(take_rows[s], low)

    def table(i):
        return tabs[2 * i], tabs[2 * i + 1]

    def right(re, im, a, b):
        mid = dot3(split(re + im), table(0))
        return mid - dot3(split(im), table(b)), mid - dot3(split(re), table(a))

    def left(re, im, a, b):
        mid = dot3(table(0), split(re + im))
        return mid - dot3(table(b), split(im)), mid - dot3(table(a), split(re))

    def send_inten(s, d):
        return remote(
            inten.at[s], inten_in.at[s, d - 1], int_sem.at[0, s, d - 1],
            int_sem.at[1, s, d - 1], mode=lax.rem(mode + d, nm),
        )

    for s in range(slots):

        def forward(k, carry):
            pr, pi = pf[k, 0], pf[k, 1]
            qr, qi = q[s, 0], q[s, 1]
            yr, yi = right(pr * qr - pi * qi, pr * qi + pi * qr, 1, 2)
            zr, zi = left(yr, yi, 1, 2)
            spec[s, k, 0] = zr
            spec[s, k, 1] = zi
            inten[s] += zr * zr + zi * zi
            return carry

        lax.fori_loop(0, nk, forward, 0)
        for d in range(1, nm):
            send_inten(s, d).start()

    own_meas.wait()
    send_meas.wait()

    def px_copy(k):
        return remote(
            pterm.at[k, :, sib_rows], px.at[k], px_sem.at[0, k], px_sem.at[1, k], sub=sib
        )

    not_owner = t != owner
    has_outer = jnp.logical_and(t > 0, t < n - 1)
    below = t < owner

    def part_right(c):
        return remote(
            x.at[c], p_left.at[c], part_send.at[c], pl_sem.at[c], scan=jnp.minimum(t + 1, n - 1)
        )

    def part_left(c):
        return remote(
            x.at[c], p_right.at[c], part_send.at[c], pr_sem.at[c], scan=jnp.maximum(t - 1, 0)
        )

    def total_left(c):
        return remote(
            tot.at[c], tot.at[c], tot_out.at[0, c], tot_in.at[c], scan=jnp.maximum(t - 1, 0)
        )

    def total_right(c):
        return remote(
            tot.at[c], tot.at[c], tot_out.at[1, c], tot_in.at[c], scan=jnp.minimum(t + 1, n - 1)
        )

    def send_part(c):
        @pl.when(below)
        def _():
            part_right(c).start()

        @pl.when(t > owner)
        def _():
            part_left(c).start()

    def ready(k):
        px_copy(k).wait_recv()
        for c in range(2):
            x[2 * k + c] = pterm[k, c, own_rows] + px[k, c]

        @pl.when(jnp.logical_and(not_owner, jnp.logical_not(has_outer)))
        def _():
            for c in range(2):
                send_part(2 * k + c)

    for s in range(slots):
        for d in range(1, nm):
            send_inten(s, d).wait_recv()
        total = inten[s]
        for d in range(1, nm):
            total = total + inten_in[s, d - 1]
        inten_in[s, 0] = live[s] * (1.0 - jnp.sqrt(mf[s] + 1.0) * lax.rsqrt(total + 1.0))

        def backward(k, carry):
            scale = inten_in[s, 0]
            yr, yi = left(spec[s, k, 0] * scale, spec[s, k, 1] * scale, 2, 1)
            cr, ci = right(yr, yi, 2, 1)
            pr, pi = pf[k, 0], pf[k, 1]
            qr, qi = q[s, 0], q[s, 1]
            objt[s, 0] += pr * cr + pi * ci
            objt[s, 1] += pr * ci - pi * cr
            tr = qr * cr + qi * ci
            ti = qr * ci - qi * cr
            if s == 0:
                pterm[k, 0] = tr
                pterm[k, 1] = ti
            else:
                pterm[k, 0] += tr
                pterm[k, 1] += ti
            if s == slots - 1:
                px_copy(k).start()

                @pl.when(k > 0)
                def _():
                    ready(k - 1)

            return carry

        lax.fori_loop(0, nk, backward, 0)

    ready(nk - 1)

    for c in range(2):
        placed = []
        for s in range(slots):
            high, low = split(objt[s, c])
            placed.append(mm(put_rows[s], high) + mm(put_rows[s], low))
        high, low = split(jnp.concatenate(placed, axis=1))
        g[c] = mm_t(high, take_cols[...]) + mm_t(low, take_cols[...])

    spans = (pl.ds(tile, HALO), pl.ds(0, tile))

    def block(m, s):
        return pl.ds(pl.multiple_of((m * 2 + s) * width, width), width)

    def sib_send(m, e):
        return remote(
            g.at[:, spans[e], block(m, sib)], g_in.at[m, :, spans[e]],
            gs_sem.at[0, m, e], gs_sem.at[1, m, e], sub=sib,
        )

    def mode_send(d, e):
        m = lax.rem(mode + d, nm)
        return remote(
            h.at[m, :, spans[e]], h_in.at[d - 1, :, spans[e]],
            hs_sem.at[0, d - 1, e], hs_sem.at[1, d - 1, e], mode=m,
        )

    edge = remote(
        h.at[mode, :, spans[0]], hz, hz_sem.at[0], hz_sem.at[1], scan=jnp.minimum(t + 1, n - 1)
    )

    def start_sib():
        for e in range(2):
            for m in range(nm):
                sib_send(m, e).start()

    def sum_sib():
        for e in range(2):
            for m in range(nm):
                sib_send(m, e).wait_recv()
                h[m, :, spans[e]] = g[:, spans[e], block(m, sub)] + g_in[m, :, spans[e]]
            for d in range(1, nm):
                mode_send(d, e).start()

    def sum_mode(e):
        for d in range(1, nm):
            mode_send(d, e).wait_recv()
        whole = h[mode, :, spans[e]]
        for d in range(1, nm):
            whole = whole + h_in[d - 1, :, spans[e]]
        if e == 0:
            h[mode, :, spans[e]] = whole

            @pl.when(t < n - 1)
            def _():
                edge.start()
        else:
            og[...] = whole

    def inward(c):
        @pl.when(jnp.logical_and(not_owner, has_outer))
        def _():
            @pl.when(below)
            def _():
                part_right(c).wait_recv()
                x[c] += p_left[c]

            @pl.when(t > owner)
            def _():
                part_left(c).wait_recv()
                x[c] += p_right[c]

            send_part(c)

        @pl.when(t == owner)
        def _():
            if owner > 0:
                part_right(c).wait_recv()
                x[c] += p_left[c]
            if owner < n - 1:
                part_left(c).wait_recv()
                x[c] += p_right[c]
            tot[c] = x[c] * (1.0 / n)
            if owner > 0:
                total_left(c).start()
            if owner < n - 1:
                total_right(c).start()
            pg[c // 2, c % 2] = tot[c]

    def outward(c):
        @pl.when(not_owner)
        def _():
            total_left(c).wait_recv()

            @pl.when(jnp.logical_and(below, t > 0))
            def _():
                total_left(c).start()

            @pl.when(jnp.logical_and(t > owner, t < n - 1))
            def _():
                total_right(c).start()

            pg[c // 2, c % 2] = tot[c]

    start_sib()
    inward(0)
    sum_sib()
    lag = 2
    for c in range(1, chunks + lag):
        if c < chunks:
            inward(c)
        if c >= lag:
            outward(c - lag)
        if c == chunks // 2:
            sum_mode(0)
    sum_mode(1)

    @pl.when(t > 0)
    def _():
        edge.wait_recv()
        og[:, pl.ds(0, HALO)] += hz[...]

    @pl.when(t > 0)
    def _():
        halo(0).wait_send()
        halo(1).wait_send()

    @pl.when(t < n - 1)
    def _():
        edge.wait_send()

    for s in range(slots):
        for d in range(1, nm):
            send_inten(s, d).wait_send()
    for k in range(nk):
        px_copy(k).wait_send()
    for e in range(2):
        for m in range(nm):
            sib_send(m, e).wait_send()
        for d in range(1, nm):
            mode_send(d, e).wait_send()
    for c in range(chunks):

        @pl.when(not_owner)
        def _():
            part_right(c).wait_send()

        @pl.when(jnp.logical_and(t <= owner, t > 0))
        def _():
            total_left(c).wait_send()

        @pl.when(jnp.logical_and(t >= owner, t < n - 1))
        def _():
            total_right(c).wait_send()


def local(n, nm, object_field, probe, offsets, counts, measured):
    f32 = jnp.float32
    tile, obj_c = object_field.shape[1:]
    nk, _, cut, frame = probe.shape
    slots = offsets.shape[1] // 2
    width = obj_c // (2 * nm)
    rows = tile + HALO
    chunks = 2 * nk
    dma = pltpu.SemaphoreType.DMA
    vmem = pl.BlockSpec(memory_space=pltpu.VMEM)
    hbm = pl.BlockSpec(memory_space=pl.ANY)
    peers = nm - 1
    tables = jnp.asarray(transform_tables(frame))
    picks = selectors(
        offsets, counts, lax.axis_index("scan") * tile, lax.axis_index("sub") * slots,
        slots, frame, tile, obj_c,
    )
    return pl.pallas_call(
        functools.partial(kernel, n, nm),
        out_shape=(
            jax.ShapeDtypeStruct((2, tile, width), f32),
            jax.ShapeDtypeStruct((nk, 2, cut, frame), f32),
        ),
        in_specs=[hbm, hbm, vmem, vmem, vmem, vmem, hbm, vmem],
        out_specs=(vmem, vmem),
        scratch_shapes=[
            pltpu.VMEM((2, rows, obj_c), f32),
            pltpu.VMEM((nk, 2, frame, frame), f32),
            pltpu.VMEM((slots, frame, frame), f32),
            pltpu.VMEM((slots, 2, frame, frame), f32),
            pltpu.VMEM((slots, nk, 2, frame, frame), f32),
            pltpu.VMEM((slots, frame, frame), f32),
            pltpu.VMEM((slots, peers, frame, frame), f32),
            pltpu.VMEM((slots, 2, frame, frame), f32),
            pltpu.VMEM((nk, 2, frame, frame), f32),
            pltpu.VMEM((nk, 2, cut, frame), f32),
            pltpu.VMEM((chunks, cut, frame), f32),
            pltpu.VMEM((chunks, cut, frame), f32),
            pltpu.VMEM((chunks, cut, frame), f32),
            pltpu.VMEM((chunks, cut, frame), f32),
            pltpu.VMEM((2, rows, obj_c), f32),
            pltpu.VMEM((nm, 2, rows, width), f32),
            pltpu.VMEM((nm, 2, rows, width), f32),
            pltpu.VMEM((peers, 2, rows, width), f32),
            pltpu.VMEM((2, HALO, width), f32),
            dma((3,)),
            dma((2,)),
            dma((2,)),
            dma((2, 2)),
            dma((2, 2)),
            dma((2, slots, peers)),
            dma((2, nk)),
            dma((chunks,)),
            dma((chunks,)),
            dma((chunks,)),
            dma((2, chunks)),
            dma((chunks,)),
            dma((2, nm, 2)),
            dma((2, peers, 2)),
            dma((2,)),
        ],
        compiler_params=pltpu.CompilerParams(
            collective_id=0, has_side_effects=True, vmem_limit_bytes=56 * 1024 * 1024
        ),
    )(object_field, probe, *picks, measured, tables)


def solution(mesh):
    in_specs = (
        P(None, ("groups", "scan"), None),
        P("mode", None, "sub", None),
        P(("groups", "scan"), None, None),
        P(("groups", "scan")),
        P(("groups", "scan"), None, None, "sub"),
    )
    out_specs = (
        P(None, ("groups", "scan"), ("mode", "sub")),
        P(("groups", "mode"), None, "sub", None),
    )
    body = functools.partial(local, mesh.shape["scan"], mesh.shape["mode"])
    return jax.shard_map(body, mesh=mesh, in_specs=in_specs, out_specs=out_specs, check_vma=False)
```

```python
import functools
import math

import jax
import jax.numpy as jnp
import numpy as np
from jax import lax
from jax.experimental import pallas as pl
from jax.experimental.pallas import tpu as pltpu
from jax.sharding import PartitionSpec as P

HALO = 128
CUTS = 1
UNROLL = 2
MESH = pl.DeviceIdType.MESH


def split_table(table):
    high = table.astype(np.float32).astype(jnp.bfloat16)
    low = (table - high.astype(np.float64)).astype(np.float32).astype(jnp.bfloat16)
    return high, low


def transform_tables(length):
    index = np.arange(length)
    angles = (index[:, None] * index[None, :] % length) * (2.0 * math.pi / length)
    cosine = np.cos(angles) / math.sqrt(length)
    sine = np.sin(angles) / math.sqrt(length)
    parts = []
    for table in (cosine, cosine + sine, cosine - sine):
        parts.extend(split_table(table))
    return np.stack(parts)


def split(x):
    high = x.astype(jnp.bfloat16)
    low = (x - high.astype(jnp.float32)).astype(jnp.bfloat16)
    return high, low


def mm(a, b):
    return jnp.dot(a, b, preferred_element_type=jnp.float32)


def mm_t(a, b):
    return lax.dot_general(a, b, (((1,), (1,)), ((), ())), preferred_element_type=jnp.float32)


def dot3(a, b):
    return mm(a[0], b[0]) + (mm(a[1], b[0]) + mm(a[0], b[1]))


def selectors(offsets, counts, tile_start, first, slots, frame):
    own = lax.dynamic_slice_in_dim(offsets[0], first, slots, axis=0)
    pixel = jnp.arange(frame, dtype=jnp.int32)
    length = slots * frame
    col = (own[:, 1:] + pixel).reshape(1, length)
    row = jnp.broadcast_to(own[:, :1] - tile_start, (slots, length))
    slot = first + jnp.arange(slots, dtype=jnp.int32)
    live = jnp.broadcast_to((slot < counts[0]).astype(jnp.int32)[:, None], (slots, length))
    return jnp.concatenate([col, row, live])


def ones_where(mask):
    return jnp.where(mask, 1.0, 0.0).astype(jnp.bfloat16)


def kernel(
    n, nm, obj, probe, sel, meas, tabs, og, pg,
    ext, pf, mf, q, spec, inten, inten_in, objt, pterm, px, x, p_left, p_right, tot,
    g, g_in, h, h_in, hz, take_rows, put_rows, take_cols, picked,
    loc_sem, probe_sem, meas_sem, halo_sem, across_sem, fwd_sem, int_sem, px_sem, part_send, pl_sem, pr_sem,
    tot_out, tot_in, gs_sem, hs_sem, hz_sem,
):
    t = lax.axis_index("scan")
    mode = lax.axis_index("mode")
    sub = lax.axis_index("sub")
    sib = 1 - sub
    tile = obj.shape[1]
    obj_c = obj.shape[2]
    nk = probe.shape[0]
    cut = probe.shape[2]
    frame = probe.shape[3]
    mcols = meas.shape[3]
    slots = mf.shape[0]
    width = og.shape[2]
    chunks = x.shape[0]
    near = n // 2 - 1

    def remote(src, dst, send, recv, **where):
        return pltpu.make_async_remote_copy(
            src_ref=src, dst_ref=dst, send_sem=send, recv_sem=recv,
            device_id=where, device_id_type=MESH,
        )

    barrier = pltpu.get_barrier_semaphore()
    pl.semaphore_signal(barrier, inc=1, device_id={"sub": sib}, device_id_type=MESH)
    for d in range(1, nm):
        pl.semaphore_signal(
            barrier, inc=1, device_id={"mode": lax.rem(mode + d, nm)}, device_id_type=MESH
        )

    @pl.when(t > 0)
    def _():
        pl.semaphore_signal(barrier, inc=1, device_id={"scan": t - 1}, device_id_type=MESH)

    @pl.when(t < n - 1)
    def _():
        pl.semaphore_signal(barrier, inc=1, device_id={"scan": t + 1}, device_id_type=MESH)

    own_obj = pltpu.make_async_copy(obj, ext.at[:, pl.ds(0, tile)], loc_sem.at[0])
    own_rows = pl.ds(pl.multiple_of(sub * cut, cut), cut)
    sib_rows = pl.ds(pl.multiple_of(sib * cut, cut), cut)
    own_probe = pltpu.make_async_copy(probe, pf.at[:, :, own_rows], loc_sem.at[1])
    own_mcols = pl.ds(pl.multiple_of(sub * mcols, mcols), mcols)
    own_meas = pltpu.make_async_copy(
        meas.at[0, pl.ds(sub * slots, slots)], mf.at[:, :, own_mcols], loc_sem.at[2]
    )
    own_obj.start()
    own_probe.start()
    own_meas.start()
    pl.semaphore_wait(
        barrier, nm + (t > 0).astype(jnp.int32) + (t < n - 1).astype(jnp.int32)
    )

    def block(m, s):
        return pl.ds(pl.multiple_of((m * 2 + s) * width, width), width)

    def halo(c):
        return remote(
            obj.at[c, pl.ds(0, HALO), block(mode, sub)],
            ext.at[c, pl.ds(tile, HALO), block(mode, sub)],
            halo_sem.at[0, c], halo_sem.at[1, c], scan=jnp.maximum(t - 1, 0),
        )

    def across(c, d):
        part = ext.at[c, pl.ds(tile, HALO), block(mode, sub)]
        return remote(
            part, part, across_sem.at[0, c, d - 1], across_sem.at[1, c, d - 1],
            mode=lax.rem(mode + d, nm),
        )

    def across_in(c, d):
        part = ext.at[c, pl.ds(tile, HALO), block(lax.rem(mode + nm - d, nm), sub)]
        return remote(
            part, part, across_sem.at[0, c, d - 1], across_sem.at[1, c, d - 1],
            mode=lax.rem(mode + d, nm),
        )

    def forwarded(c, d, s):
        part = ext.at[c, pl.ds(tile, HALO), block(lax.rem(mode + nm - d, nm), s)]
        return remote(part, part, fwd_sem.at[0, c, d], fwd_sem.at[1, c, d], sub=sib)

    @pl.when(t > 0)
    def _():
        halo(0).start()
        halo(1).start()

    send_probe = remote(
        probe, pf.at[:, :, own_rows], probe_sem.at[0], probe_sem.at[1], sub=sib
    )
    send_probe.start()
    send_meas = remote(
        meas.at[0, pl.ds(sib * slots, slots)], mf.at[:, :, own_mcols],
        meas_sem.at[0], meas_sem.at[1], sub=sib,
    )
    send_meas.start()

    def iota(shape, axis):
        return lax.broadcasted_iota(jnp.int32, shape, axis)

    rows = tile + HALO
    take_cols[...] = ones_where(iota((obj_c, slots * frame), 0) == sel[0:1])
    for s in range(slots):
        first = sel[1 + s : 2 + s]
        take_rows[s] = ones_where(
            iota((frame, rows), 1) - iota((frame, rows), 0) == first[:, :rows]
        )
        put_rows[s] = ones_where(
            iota((rows, frame), 0) - iota((rows, frame), 1) == first[:, :frame]
        )
    own_obj.wait()

    def pick(c, at, count):
        high, low = split(ext[c, pl.ds(at, count)])
        picked[c, pl.ds(at, count)] = mm(high, take_cols[...]) + mm(low, take_cols[...])

    for c in range(2):
        pick(c, 0, tile)
    objt[...] = jnp.zeros_like(objt)
    inten[...] = jnp.zeros_like(inten)

    @pl.when(t < n - 1)
    def _():
        for c in range(2):
            halo(c).wait_recv()
            for d in range(1, nm):
                across(c, d).start()
            forwarded(c, 0, sub).start()
        for c in range(2):
            for d in range(1, nm):
                across_in(c, d).wait_recv()
                forwarded(c, d, sub).start()
        for c in range(2):
            for d in range(nm):
                forwarded(c, d, sib).wait_recv()
                forwarded(c, d, sub).wait_send()
            for d in range(1, nm):
                across(c, d).wait_send()

    @pl.when(t == n - 1)
    def _():
        ext[:, pl.ds(tile, HALO)] = jnp.zeros((2, HALO, obj_c), jnp.float32)

    own_probe.wait()
    send_probe.wait()

    for c in range(2):
        pick(c, tile, HALO)
        for s in range(slots):
            high, low = split(picked[c, :, s * frame : (s + 1) * frame])
            q[s, c] = mm(take_rows[s], high) + mm(take_rows[s], low)

    def table(i):
        return tabs[2 * i], tabs[2 * i + 1]

    def right(re, im, a, b):
        mid = dot3(split(re + im), table(0))
        return mid - dot3(split(im), table(b)), mid - dot3(split(re), table(a))

    def left(re, im, a, b):
        mid = dot3(table(0), split(re + im))
        return mid - dot3(table(b), split(im)), mid - dot3(table(a), split(re))

    def send_inten(s, d):
        return remote(
            inten.at[s], inten_in.at[s, d - 1], int_sem.at[0, s, d - 1],
            int_sem.at[1, s, d - 1], mode=lax.rem(mode + d, nm),
        )

    for s in range(slots):

        def forward(k, carry):
            pr, pi = pf[k, 0], pf[k, 1]
            qr, qi = q[s, 0], q[s, 1]
            yr, yi = right(pr * qr - pi * qi, pr * qi + pi * qr, 1, 2)
            zr, zi = left(yr, yi, 1, 2)
            spec[s, k, 0] = zr
            spec[s, k, 1] = zi
            inten[s] += zr * zr + zi * zi
            return carry

        lax.fori_loop(0, nk, forward, 0, unroll=UNROLL)
        for d in range(1, nm):
            send_inten(s, d).start()

    own_meas.wait()
    send_meas.wait()

    def px_copy(k):
        return remote(
            pterm.at[k, :, sib_rows], px.at[k], px_sem.at[0, k], px_sem.at[1, k], sub=sib
        )

    middle = jnp.logical_or(t == near, t == near + 1)
    has_outer = jnp.logical_and(t > 0, t < n - 1)
    below = t <= near
    send_total_left = jnp.logical_and(below, t > 0)
    send_total_right = jnp.logical_and(t > near, t < n - 1)

    def part_right(c):
        return remote(
            x.at[c], p_left.at[c], part_send.at[c], pl_sem.at[c], scan=jnp.minimum(t + 1, n - 1)
        )

    def part_left(c):
        return remote(
            x.at[c], p_right.at[c], part_send.at[c], pr_sem.at[c], scan=jnp.maximum(t - 1, 0)
        )

    def total_left(c):
        return remote(
            tot.at[c], tot.at[c], tot_out.at[0, c], tot_in.at[c], scan=jnp.maximum(t - 1, 0)
        )

    def total_right(c):
        return remote(
            tot.at[c], tot.at[c], tot_out.at[1, c], tot_in.at[c], scan=jnp.minimum(t + 1, n - 1)
        )

    def send_part(c):
        @pl.when(below)
        def _():
            part_right(c).start()

        @pl.when(t > near)
        def _():
            part_left(c).start()

    def ready(k):
        px_copy(k).wait_recv()
        for c in range(2):
            for i in range(CUTS):
                at = i * (cut // CUTS)
                part = pl.ds(pl.multiple_of(sub * cut + at, cut // CUTS), cut // CUTS)
                x[(2 * k + c) * CUTS + i] = pterm[k, c, part] + px[k, c, pl.ds(at, cut // CUTS)]

        @pl.when(jnp.logical_not(has_outer))
        def _():
            for c in range(2 * CUTS):
                send_part(2 * CUTS * k + c)

    for s in range(slots):
        for d in range(1, nm):
            send_inten(s, d).wait_recv()
        total = inten[s]
        for d in range(1, nm):
            total = total + inten_in[s, d - 1]
        live = sel[1 + slots + s : 2 + slots + s, :frame].astype(jnp.float32)
        inten_in[s, 0] = live * (1.0 - jnp.sqrt(mf[s] + 1.0) * lax.rsqrt(total + 1.0))

        def backward(k, carry):
            scale = inten_in[s, 0]
            yr, yi = left(spec[s, k, 0] * scale, spec[s, k, 1] * scale, 2, 1)
            cr, ci = right(yr, yi, 2, 1)
            pr, pi = pf[k, 0], pf[k, 1]
            qr, qi = q[s, 0], q[s, 1]
            objt[s, 0] += pr * cr + pi * ci
            objt[s, 1] += pr * ci - pi * cr
            tr = qr * cr + qi * ci
            ti = qr * ci - qi * cr
            if s == 0:
                pterm[k, 0] = tr
                pterm[k, 1] = ti
            else:
                pterm[k, 0] += tr
                pterm[k, 1] += ti
            if s == slots - 1:
                px_copy(k).start()

                @pl.when(k > 0)
                def _():
                    ready(k - 1)

            return carry

        lax.fori_loop(0, nk, backward, 0, unroll=UNROLL)

    ready(nk - 1)

    for c in range(2):
        placed = []
        for s in range(slots):
            high, low = split(objt[s, c])
            placed.append(mm(put_rows[s], high) + mm(put_rows[s], low))
        high, low = split(jnp.concatenate(placed, axis=1))
        g[c] = mm_t(high, take_cols[...]) + mm_t(low, take_cols[...])

    spans = (pl.ds(tile, HALO), pl.ds(0, tile))

    def sib_send(m, e):
        return remote(
            g.at[:, spans[e], block(m, sib)], g_in.at[m, :, spans[e]],
            gs_sem.at[0, m, e], gs_sem.at[1, m, e], sub=sib,
        )

    def mode_send(d, e):
        m = lax.rem(mode + d, nm)
        return remote(
            h.at[m, :, spans[e]], h_in.at[d - 1, :, spans[e]],
            hs_sem.at[0, d - 1, e], hs_sem.at[1, d - 1, e], mode=m,
        )

    edge = remote(
        h.at[mode, :, spans[0]], hz, hz_sem.at[0], hz_sem.at[1], scan=jnp.minimum(t + 1, n - 1)
    )

    order = [lax.rem(mode + d, nm) for d in range(1, nm)] + [mode]

    def start_sib():
        for m in order:
            for e in range(2):
                sib_send(m, e).start()

    def sum_sib():
        for d, m in enumerate(order, 1):
            for e in range(2):
                sib_send(m, e).wait_recv()
                h[m, :, spans[e]] = g[:, spans[e], block(m, sub)] + g_in[m, :, spans[e]]
                if d < nm:
                    mode_send(d, e).start()

    def sum_mode(e):
        for d in range(1, nm):
            mode_send(d, e).wait_recv()
        whole = h[mode, :, spans[e]]
        for d in range(1, nm):
            whole = whole + h_in[d - 1, :, spans[e]]
        if e == 0:
            h[mode, :, spans[e]] = whole

            @pl.when(t < n - 1)
            def _():
                edge.start()
        else:
            og[...] = whole

    def inward(c):
        @pl.when(has_outer)
        def _():
            @pl.when(below)
            def _():
                part_right(c).wait_recv()
                x[c] += p_left[c]

            @pl.when(t > near)
            def _():
                part_left(c).wait_recv()
                x[c] += p_right[c]

            send_part(c)

    def finish(c):
        @pl.when(t == near)
        def _():
            part_left(c).wait_recv()
            tot[c] = (x[c] + p_right[c]) * (1.0 / n)

        @pl.when(t == near + 1)
        def _():
            part_right(c).wait_recv()
            tot[c] = (x[c] + p_left[c]) * (1.0 / n)

        @pl.when(jnp.logical_not(middle))
        def _():
            total_left(c).wait_recv()

        @pl.when(send_total_left)
        def _():
            total_left(c).start()

        @pl.when(send_total_right)
        def _():
            total_right(c).start()

        at = c % CUTS * (cut // CUTS)
        pg[c // (2 * CUTS), c // CUTS % 2, pl.ds(at, cut // CUTS)] = tot[c]

    start_sib()
    inward(0)
    inward(1)
    sum_sib()
    lag = 2
    for c in range(2, chunks + lag):
        if c < chunks:
            inward(c)
        finish(c - lag)
        if c == max(2, chunks // 2):
            sum_mode(0)
    sum_mode(1)

    @pl.when(t > 0)
    def _():
        edge.wait_recv()
        og[:, pl.ds(0, HALO)] += hz[...]

    @pl.when(t > 0)
    def _():
        halo(0).wait_send()
        halo(1).wait_send()

    @pl.when(t < n - 1)
    def _():
        edge.wait_send()

    for s in range(slots):
        for d in range(1, nm):
            send_inten(s, d).wait_send()
    for k in range(nk):
        px_copy(k).wait_send()
    for e in range(2):
        for m in range(nm):
            sib_send(m, e).wait_send()
        for d in range(1, nm):
            mode_send(d, e).wait_send()
    for c in range(chunks):

        part_right(c).wait_send()

        @pl.when(send_total_left)
        def _():
            total_left(c).wait_send()

        @pl.when(send_total_right)
        def _():
            total_right(c).wait_send()


def local(n, nm, object_field, probe, offsets, counts, measured):
    f32 = jnp.float32
    tile, obj_c = object_field.shape[1:]
    nk, _, cut, frame = probe.shape
    slots = offsets.shape[1] // 2
    width = obj_c // (2 * nm)
    rows = tile + HALO
    chunks = 2 * nk * CUTS
    dma = pltpu.SemaphoreType.DMA
    vmem = pl.BlockSpec(memory_space=pltpu.VMEM)
    hbm = pl.BlockSpec(memory_space=pl.ANY)
    peers = nm - 1
    tables = jnp.asarray(transform_tables(frame))
    picks = selectors(
        offsets, counts, lax.axis_index("scan") * tile, lax.axis_index("sub") * slots,
        slots, frame,
    )
    return pl.pallas_call(
        functools.partial(kernel, n, nm),
        out_shape=(
            jax.ShapeDtypeStruct((2, tile, width), f32),
            jax.ShapeDtypeStruct((nk, 2, cut, frame), f32),
        ),
        in_specs=[hbm, hbm, vmem, hbm, vmem],
        out_specs=(vmem, vmem),
        scratch_shapes=[
            pltpu.VMEM((2, rows, obj_c), f32),
            pltpu.VMEM((nk, 2, frame, frame), f32),
            pltpu.VMEM((slots, frame, frame), f32),
            pltpu.VMEM((slots, 2, frame, frame), f32),
            pltpu.VMEM((slots, nk, 2, frame, frame), f32),
            pltpu.VMEM((slots, frame, frame), f32),
            pltpu.VMEM((slots, peers, frame, frame), f32),
            pltpu.VMEM((slots, 2, frame, frame), f32),
            pltpu.VMEM((nk, 2, frame, frame), f32),
            pltpu.VMEM((nk, 2, cut, frame), f32),
            pltpu.VMEM((chunks, cut // CUTS, frame), f32),
            pltpu.VMEM((chunks, cut // CUTS, frame), f32),
            pltpu.VMEM((chunks, cut // CUTS, frame), f32),
            pltpu.VMEM((chunks, cut // CUTS, frame), f32),
            pltpu.VMEM((2, rows, obj_c), f32),
            pltpu.VMEM((nm, 2, rows, width), f32),
            pltpu.VMEM((nm, 2, rows, width), f32),
            pltpu.VMEM((peers, 2, rows, width), f32),
            pltpu.VMEM((2, HALO, width), f32),
            pltpu.VMEM((slots, frame, rows), jnp.bfloat16),
            pltpu.VMEM((slots, rows, frame), jnp.bfloat16),
            pltpu.VMEM((obj_c, slots * frame), jnp.bfloat16),
            pltpu.VMEM((2, rows, slots * frame), f32),
            dma((3,)),
            dma((2,)),
            dma((2,)),
            dma((2, 2)),
            dma((2, 2, peers)),
            dma((2, 2, nm)),
            dma((2, slots, peers)),
            dma((2, nk)),
            dma((chunks,)),
            dma((chunks,)),
            dma((chunks,)),
            dma((2, chunks)),
            dma((chunks,)),
            dma((2, nm, 2)),
            dma((2, peers, 2)),
            dma((2,)),
        ],
        compiler_params=pltpu.CompilerParams(
            collective_id=0, has_side_effects=True, vmem_limit_bytes=56 * 1024 * 1024
        ),
    )(object_field, probe, picks, measured, tables)


def solution(mesh):
    in_specs = (
        P(None, ("groups", "scan"), None),
        P("mode", None, "sub", None),
        P(("groups", "scan"), None, None),
        P(("groups", "scan")),
        P(("groups", "scan"), None, None, "sub"),
    )
    out_specs = (
        P(None, ("groups", "scan"), ("mode", "sub")),
        P(("groups", "mode"), None, "sub", None),
    )
    body = functools.partial(local, mesh.shape["scan"], mesh.shape["mode"])
    return jax.shard_map(body, mesh=mesh, in_specs=in_specs, out_specs=out_specs, check_vma=False)
```
